256 devices in a mesh: leaf: 64 (over x, z, core), blk: 4 (over y).
Axes of the slice: x: 4, y: 4, z: 8, core: 2. Of those that a mesh axis runs over, the one named last changes fastest.
Arguments:
- sources: bfloat16 [128, 1048576], P(None, ('leaf', 'blk')), may hold values from -6 to 6
- near_blocks: bfloat16 [8192, 6, 128, 128], P(('leaf', 'blk')), may hold values from -0.21875 to 0.21875
- near_cols: int32 [8192, 6], P(('leaf', 'blk')), may hold values from 0 to 8191, as said below
- basis: bfloat16 [8192, 64, 128], P(('leaf', 'blk')), may hold values from -0.046875 to 0.046875
- transfer: bfloat16 [126, 64, 64], replicated, may hold values from -0.75 to 0.75
- coupling: bfloat16 [126, 64, 64], replicated, may hold values from -0.75 to 0.75
Outputs:
- potential: float32 [128, 1048576], P(None, ('leaf', 'blk'))
The draws below stay inside these ranges and needn't reach their ends.
Inputs may be any that keep to these rules, and one draw needn't show every extreme that they name: `near_cols`: for cluster c the entries are c, min(c + 4, 8191), max(c - 4, 0), then entries within 4 clusters of c, clipped to the grid of clusters.
All inputs are finite; a program needn't handle non-finite values.
Results may differ from the reference program's by a relative error of at most 0.0012.
Values may be sent and summed in bfloat16 or wider, within the bound.
No kernel may reach another device: no remote copies, remote signals or barrier semaphores. Data moves between devices by JAX's collectives and lax.ppermute only.
A program may use at most 128 MiB of HBM per device.

```python
import jax
import jax.numpy as jnp
from jax import lax

PANEL = 128
RANK = 64
NEAR = 6
REACH = 4
CL_DEV = 32
RHS = 128
CLUSTERS = 8192
PANELS = 1048576
N_LEAF = 64
N_BLK = 4


def draw_near_cols(key, part):
    rows = jnp.arange(CLUSTERS, dtype=jnp.int32)[:, None]
    fixed_offsets = jnp.array([0, REACH, -REACH], dtype=jnp.int32)[None, :] * jnp.ones((CLUSTERS, 1), jnp.int32)
    random_offsets = jax.random.randint(key, (CLUSTERS, NEAR - 3), -REACH, REACH + 1).astype(jnp.int32)
    offsets = jnp.concatenate([fixed_offsets, random_offsets], axis=1)
    return jnp.clip(rows + offsets, 0, CLUSTERS - 1).astype(jnp.int32)


def level_of(rng, shape, split, low, top_value):
    level = 1.0
    for dim, blocks in split:
        steps = jax.random.uniform(jax.random.fold_in(jax.random.fold_in(rng, 6), dim), (blocks,), jnp.float32, low / len(split), top_value / len(split))
        level = level * jnp.repeat(jnp.exp(steps), shape[dim] // blocks).reshape((-1,) + (1,) * (len(shape) - 1 - dim))
    return level


def scatter_about(key, extent, width, bound, pieces=(), kind=jnp.bfloat16):
    values = jax.random.normal(key, extent, jnp.float32) * width
    if len(pieces) > 0:
        values = level_of(key, extent, pieces, -0.22, 0.18) * values
    return jnp.clip(values, min=-bound, max=bound).astype(kind)


def setup_inputs(seed: int = 0) -> dict:
    streams_of = jax.random.split(jax.random.key(seed), 7)
    return {
        "sources": scatter_about(streams_of[0], (RHS, PANELS), 1.0, 6.0, ((1, 256),)),
        "near_blocks": scatter_about(streams_of[1], (CLUSTERS, NEAR, PANEL, PANEL), (NEAR * PANEL) ** -0.5, 0.21875, ((0, 256),)),
        "near_cols": draw_near_cols(jax.random.fold_in(streams_of[6], 71), 0),
        "basis": scatter_about(streams_of[3], (CLUSTERS, RANK, PANEL), (N_BLK * CL_DEV * PANEL) ** -0.5, 0.046875, ((0, 256),)),
        "transfer": scatter_about(streams_of[4], (2 * N_LEAF - 2, RANK, RANK), RANK ** -0.5, 0.75),
        "coupling": scatter_about(streams_of[5], (2 * N_LEAF - 2, RANK, RANK), RANK ** -0.5, 0.75),
    }


highest = lax.Precision.HIGHEST


def reference(sources, near_blocks, near_cols, basis, transfer, coupling):
    levels = int(N_LEAF).bit_length() - 1
    devices_all = N_LEAF * N_BLK
    group_clusters = CL_DEV * N_BLK
    cluster_sources = sources.reshape(RHS, CLUSTERS, PANEL)

    def near_piece(start_row):
        columns = lax.dynamic_slice_in_dim(near_cols, start_row, CL_DEV, 0)
        blocks = lax.dynamic_slice_in_dim(near_blocks, start_row, CL_DEV, 0)
        picked = jnp.take(cluster_sources, columns, axis=1)
        return jnp.einsum("rcjp,cjpq->rcq", picked.astype(jnp.float32), blocks.astype(jnp.float32))

    starts = (jnp.arange(devices_all) * CL_DEV).astype(jnp.int32)
    near = lax.map(near_piece, starts)
    near = jnp.transpose(near, (1, 0, 2, 3)).reshape(RHS, CLUSTERS, PANEL)

    terms = jnp.einsum("rcp,ckp->rck", cluster_sources.astype(jnp.float32), basis.astype(jnp.float32))
    leaf_moments = jnp.transpose(terms.reshape(RHS, N_LEAF, group_clusters, RANK).sum(axis=2), (1, 0, 2))

    upward = [leaf_moments]
    current = leaf_moments
    for level in range(levels - 1):
        node_count = N_LEAF >> level
        matrices = transfer[node_count - 2:2 * node_count - 2].astype(jnp.float32)
        moved = jnp.einsum("nrk,nkj->nrj", current, matrices, precision=highest)
        current = moved.reshape(node_count // 2, 2, RHS, RANK).sum(axis=1)
        upward.append(current)

    local_terms = []
    for level in range(levels):
        node_count = N_LEAF >> level
        paired = upward[level].reshape(node_count // 2, 2, RHS, RANK)[:, ::-1].reshape(node_count, RHS, RANK)
        matrices = coupling[node_count - 2:2 * node_count - 2].astype(jnp.float32)
        local_terms.append(jnp.einsum("nrk,nkj->nrj", paired, matrices, precision=highest))

    descended = local_terms[levels - 1]
    for level in range(levels - 2, -1, -1):
        node_count = N_LEAF >> level
        matrices = transfer[node_count - 2:2 * node_count - 2].astype(jnp.float32)
        widened = jnp.repeat(descended, 2, axis=0)
        descended = local_terms[level] + jnp.einsum("nrj,nkj->nrk", widened, matrices, precision=highest)

    leaf_local = lax.optimization_barrier(descended.astype(jnp.bfloat16)).astype(jnp.float32)
    grouped_basis = basis.reshape(N_LEAF, group_clusters, RANK, PANEL).astype(jnp.float32)
    far = jnp.einsum("grk,gckp->rgcp", leaf_local, grouped_basis)
    return (near + far.reshape(RHS, CLUSTERS, PANEL)).reshape(RHS, PANELS)
```

```python
import functools

import jax
import jax.numpy as jnp
from jax import lax
from jax.experimental import pallas as pl
from jax.experimental.pallas import tpu as pltpu
from jax.sharding import PartitionSpec as P

REACH = 4

highest = lax.Precision.HIGHEST
AXES = ("leaf", "blk")
NT = (((1,), (1,)), ((), ()))
TN = (((0,), (0,)), ((), ()))
NN = (((1,), (0,)), ((), ()))


def xor_permute(value, axis, mask):
    pairs = [(source, source ^ mask) for source in range(lax.axis_size(axis))]
    return lax.ppermute(value, axis, pairs)


def neighbour_clusters(sources, width):
    count = lax.axis_size(AXES)
    head = sources[:, :width]
    tail = sources[:, sources.shape[1] - width :]
    left = lax.ppermute(tail, AXES, [(i, i + 1) for i in range(count - 1)])
    right = lax.ppermute(head, AXES, [(i + 1, i) for i in range(count - 1)])
    return left, right


def moment_kernel(sources_ref, basis_ref, moment_ref):
    @pl.when(pl.program_id(0) == 0)
    def _():
        moment_ref[...] = jnp.zeros_like(moment_ref)

    clusters, _, panel = basis_ref.shape
    flat = jnp.concatenate([basis_ref[c] for c in range(clusters)], axis=1)
    moment_ref[...] += lax.dot_general(
        flat, sources_ref[...], NT, preferred_element_type=jnp.float32
    )


def moments(sources, basis, steps=4):
    rhs, panels = sources.shape
    clusters, rank, panel = basis.shape
    return pl.pallas_call(
        moment_kernel,
        grid=(steps,),
        in_specs=[
            pl.BlockSpec((rhs, panels // steps), lambda i: (0, i)),
            pl.BlockSpec((clusters // steps, rank, panel), lambda i: (i, 0, 0)),
        ],
        out_specs=pl.BlockSpec((rank, rhs), lambda i: (0, 0)),
        out_shape=jax.ShapeDtypeStruct((rank, rhs), jnp.float32),
        cost_estimate=pl.CostEstimate(
            flops=2 * rhs * panels * rank, bytes_accessed=2 * panels * (rhs + rank), transcendentals=0
        ),
        name="moments",
    )(sources, basis)


def tree_kernel(levels, rows_ref, transfer_ref, coupling_ref, up_ref, down_ref, mats, sems):
    copies = []
    for level in range(levels):
        row = rows_ref[level]
        pair = rows_ref[levels + level]
        copies.append(pltpu.make_async_copy(coupling_ref.at[row], mats.at[3 * level], sems.at[3 * level]))
        if level + 1 < levels:
            copies.append(pltpu.make_async_copy(transfer_ref.at[row], mats.at[3 * level + 1], sems.at[3 * level + 1]))
            copies.append(pltpu.make_async_copy(transfer_ref.at[pair], mats.at[3 * level + 2], sems.at[3 * level + 2]))
    for copy in copies:
        copy.start()
    for copy in copies:
        copy.wait()
    chain = None
    for level in range(levels):
        couple = mats[3 * level].astype(jnp.float32)
        if chain is None:
            down_ref[level] = couple.T
        else:
            down_ref[level] = lax.dot_general(
                chain, couple, NT, precision=highest, preferred_element_type=jnp.float32
            )
        if level + 1 < levels:
            mine = mats[3 * level + 1].astype(jnp.float32)
            theirs = mats[3 * level + 2].astype(jnp.float32)
            up_ref[2 * level] = mine.T
            up_ref[2 * level + 1] = theirs.T
            if chain is None:
                chain = mine
            else:
                chain = lax.dot_general(
                    chain, mine, NN, precision=highest, preferred_element_type=jnp.float32
                )


def tree_matrices(transfer, coupling, rows, levels):
    rank = transfer.shape[1]
    any_spec = pl.BlockSpec(memory_space=pl.ANY)
    return pl.pallas_call(
        functools.partial(tree_kernel, levels),
        in_specs=[pl.BlockSpec(memory_space=pltpu.SMEM), any_spec, any_spec],
        out_specs=[pl.BlockSpec(memory_space=pltpu.VMEM)] * 2,
        out_shape=[
            jax.ShapeDtypeStruct((2 * (levels - 1), rank, rank), jnp.float32),
            jax.ShapeDtypeStruct((levels, rank, rank), jnp.float32),
        ],
        scratch_shapes=[
            pltpu.VMEM((3 * levels, rank, rank), jnp.bfloat16),
            pltpu.SemaphoreType.DMA((3 * levels,)),
        ],
        cost_estimate=pl.CostEstimate(
            flops=2 * 6 * 2 * levels * rank**3, bytes_accessed=3 * levels * rank * rank * 4, transcendentals=0
        ),
        name="tree_matrices",
    )(rows, transfer, coupling)


def near_kernel(per_step, columns_ref, sources_ref, left_ref, right_ref, blocks_ref, near_ref, extended):
    step = pl.program_id(0)
    width = left_ref.shape[1]
    panels = sources_ref.shape[1]
    near_count = blocks_ref.shape[1]
    panel = blocks_ref.shape[2]

    @pl.when(step == 0)
    def _():
        extended[:, :width] = left_ref[...]
        extended[:, width : width + panels] = sources_ref[...]
        extended[:, width + panels :] = right_ref[...]

    for c in range(per_step):
        picked = []
        for slot in range(near_count):
            column = columns_ref[(step * per_step + c) * near_count + slot]
            picked.append(extended[:, pl.ds(pl.multiple_of(column * panel, panel), panel)])
        near_ref[:, c * panel : (c + 1) * panel] = jnp.dot(
            jnp.concatenate(picked, axis=1),
            blocks_ref[c].reshape(near_count * panel, panel),
            preferred_element_type=jnp.float32,
        )


def near_field(columns, sources, left, right, blocks, per_step=4):
    rhs, panels = sources.shape
    clusters, near_count, panel, _ = blocks.shape
    width = left.shape[1]
    whole = lambda i, columns: (0, 0)
    return pl.pallas_call(
        functools.partial(near_kernel, per_step),
        grid_spec=pltpu.PrefetchScalarGridSpec(
            num_scalar_prefetch=1,
            grid=(clusters // per_step,),
            in_specs=[
                pl.BlockSpec((rhs, panels), whole),
                pl.BlockSpec((rhs, width), whole),
                pl.BlockSpec((rhs, width), whole),
                pl.BlockSpec((per_step, near_count, panel, panel), lambda i, columns: (i, 0, 0, 0)),
            ],
            out_specs=pl.BlockSpec((rhs, per_step * panel), lambda i, columns: (0, i)),
            scratch_shapes=[pltpu.VMEM((rhs, panels + 2 * width), sources.dtype)],
        ),
        out_shape=jax.ShapeDtypeStruct((rhs, panels), jnp.float32),
        compiler_params=pltpu.CompilerParams(vmem_limit_bytes=24 * 1024 * 1024),
        cost_estimate=pl.CostEstimate(
            flops=2 * rhs * panels * near_count * panel,
            bytes_accessed=2 * panels * near_count * panel + 6 * rhs * panels,
            transcendentals=0,
        ),
        name="near_field",
    )(columns, sources, left, right, blocks)


def far_kernel(partial_ref, last_ref, matrix_ref, near_ref, basis_ref, out_ref, leaf_local):
    @pl.when(pl.program_id(0) == 0)
    def _():
        descended = partial_ref[...] + lax.dot_general(
            matrix_ref[0], last_ref[...], NN, precision=highest, preferred_element_type=jnp.float32
        )
        leaf_local[...] = descended.T.astype(leaf_local.dtype)

    clusters, _, panel = basis_ref.shape
    for c in range(clusters):
        columns = slice(c * panel, (c + 1) * panel)
        out_ref[:, columns] = near_ref[:, columns] + jnp.dot(
            leaf_local[...], basis_ref[c], preferred_element_type=jnp.float32
        )


def add_far(partial, last, matrices, near, basis, steps=4):
    rhs, panels = near.shape
    clusters, rank, panel = basis.shape
    levels = matrices.shape[0]
    whole = lambda i: (0, 0)
    return pl.pallas_call(
        far_kernel,
        grid=(steps,),
        in_specs=[
            pl.BlockSpec((rank, rhs), whole),
            pl.BlockSpec((rank, rhs), whole),
            pl.BlockSpec((1, rank, rank), lambda i: (levels - 1, 0, 0)),
            pl.BlockSpec((rhs, panels // steps), lambda i: (0, i)),
            pl.BlockSpec((clusters // steps, rank, panel), lambda i: (i, 0, 0)),
        ],
        out_specs=pl.BlockSpec((rhs, panels // steps), lambda i: (0, i)),
        out_shape=jax.ShapeDtypeStruct((rhs, panels), jnp.float32),
        scratch_shapes=[pltpu.VMEM((rhs, rank), jnp.bfloat16)],
        cost_estimate=pl.CostEstimate(
            flops=2 * rhs * panels * rank, bytes_accessed=8 * rhs * panels + 2 * rank * panels, transcendentals=0
        ),
        name="add_far",
    )(partial, last, matrices, near, basis)


def matmul(left, right):
    return jnp.dot(left, right, precision=highest, preferred_element_type=jnp.float32)


def body(sources, near_blocks, near_cols, basis, transfer, coupling):
    own_clusters = near_blocks.shape[0]
    panel_size = near_blocks.shape[2]
    leaf_count = lax.axis_size("leaf")
    blk_count = lax.axis_size("blk")
    levels = leaf_count.bit_length() - 1
    leaf_index = lax.axis_index("leaf")

    left, right = neighbour_clusters(sources, REACH * panel_size)
    moment = moments(sources, basis)

    level_index = jnp.arange(levels, dtype=jnp.int32)
    node = jnp.right_shift(leaf_index, level_index)
    first_row = jnp.right_shift(leaf_count, level_index) - 2
    rows = jnp.concatenate([first_row + node, first_row + (node ^ 1)]).astype(jnp.int32)
    up, down = tree_matrices(transfer, coupling, rows, levels)

    first_cluster = lax.axis_index(AXES) * own_clusters
    columns = (near_cols - (first_cluster - REACH)).reshape(-1)
    near = near_field(columns, sources, left, right, near_blocks)

    current = moment
    for bit in range(blk_count.bit_length() - 1):
        current = current + xor_permute(current, "blk", 2 ** (bit + 1) - 1)

    masks = [1, 2, 4, 12, 16, 48]
    collected = jnp.zeros_like(moment)
    for level in range(levels):
        sibling = xor_permute(current, "leaf", masks[level])
        if level + 1 < levels:
            current = matmul(up[2 * level], current) + matmul(up[2 * level + 1], sibling)
            collected = collected + matmul(down[level], sibling)
    return add_far(collected, sibling, down, near, basis)


def solution(mesh):
    return jax.shard_map(
        body,
        mesh=mesh,
        in_specs=(
            P(None, ("leaf", "blk")),
            P(("leaf", "blk"), None, None, None),
            P(("leaf", "blk"), None),
            P(("leaf", "blk"), None, None),
            P(),
            P(),
        ),
        out_specs=P(None, ("leaf", "blk")),
        check_vma=False,
    )
```

```python
import functools

import jax
import jax.numpy as jnp
from jax import lax
from jax.experimental import pallas as pl
from jax.experimental.pallas import tpu as pltpu
from jax.sharding import PartitionSpec as P

REACH = 4
HALVES = 2
QUARTERS = 4
VMEM_BYTES = 16 * 1024 * 1024
NEAR_VMEM_BYTES = 16 * 1024 * 1024
MOMENT_VMEM_BYTES = 54784 * 1024

highest = lax.Precision.HIGHEST
AXES = ("leaf", "blk")
NT = (((1,), (1,)), ((), ()))
TN = (((0,), (0,)), ((), ()))


def xor_permute(value, axis, mask):
    pairs = [(source, source ^ mask) for source in range(lax.axis_size(axis))]
    return lax.ppermute(value, axis, pairs)


def inner_exchange(value):
    count = lax.axis_size(AXES)
    return lax.ppermute(value, AXES, [(i, i ^ 1) for i in range(count)])


def outer_exchange(value):
    count = lax.axis_size(AXES)
    pairs = [(i, i + 1) for i in range(1, count - 1, 2)]
    return lax.ppermute(value, AXES, pairs + [(b, a) for a, b in pairs])


def moment_kernel(odd_ref, sources_hbm, basis_hbm, moment_ref, inner_ref, outer_ref, sources, basis, sems):
    chunks = sources.shape[0]
    clusters = basis.shape[0] // chunks
    panels = sources.shape[2]
    width = inner_ref.shape[1]
    copies = []
    for k in range(chunks):
        own = slice(k * clusters, (k + 1) * clusters)
        copies.append(
            (
                pltpu.make_async_copy(
                    sources_hbm.at[:, k * panels : (k + 1) * panels], sources.at[k], sems.at[2 * k]
                ),
                pltpu.make_async_copy(basis_hbm.at[own], basis.at[own], sems.at[2 * k + 1]),
            )
        )
        for copy in copies[-1]:
            copy.start()
    total = jnp.zeros(moment_ref.shape, jnp.float32)
    for k in range(chunks):
        for copy in copies[k]:
            copy.wait()
        flat = jnp.concatenate([basis[k * clusters + c] for c in range(clusters)], axis=1)
        total += lax.dot_general(flat, sources[k], NT, preferred_element_type=jnp.float32)
    moment_ref[...] = total
    odd = odd_ref[0]

    @pl.when(odd == 0)
    def _():
        inner_ref[...] = sources[chunks - 1, :, panels - width :]
        outer_ref[...] = sources[0, :, :width]

    @pl.when(odd != 0)
    def _():
        inner_ref[...] = sources[0, :, :width]
        outer_ref[...] = sources[chunks - 1, :, panels - width :]


def moments(odd, sources, basis, width, chunks=4):
    rhs, panels = sources.shape
    clusters, rank, panel = basis.shape
    vmem = pl.BlockSpec(memory_space=pltpu.VMEM)
    hbm = pl.BlockSpec(memory_space=pltpu.HBM)
    return pl.pallas_call(
        moment_kernel,
        in_specs=[pl.BlockSpec(memory_space=pltpu.SMEM), hbm, hbm],
        out_specs=[vmem] * 3,
        out_shape=[
            jax.ShapeDtypeStruct((rank, rhs), jnp.float32),
            jax.ShapeDtypeStruct((rhs, width), sources.dtype),
            jax.ShapeDtypeStruct((rhs, width), sources.dtype),
        ],
        scratch_shapes=[
            pltpu.VMEM((chunks, rhs, panels // chunks), sources.dtype),
            pltpu.VMEM((clusters, rank, panel), basis.dtype),
            pltpu.SemaphoreType.DMA((2 * chunks,)),
        ],
        compiler_params=pltpu.CompilerParams(vmem_limit_bytes=MOMENT_VMEM_BYTES),
        cost_estimate=pl.CostEstimate(
            flops=2 * rhs * panels * rank, bytes_accessed=2 * panels * (rhs + rank), transcendentals=0
        ),
        name="moments",
    )(odd, sources, basis)


def near_products(columns_ref, panels_ref, near_ref, blocks_ref, first, base):
    quarter_clusters, near_count, panel, _ = blocks_ref.shape
    for c in range(quarter_clusters):
        picked = []
        for slot in range(near_count):
            column = columns_ref[slot, first + c] - base
            picked.append(panels_ref[:, pl.ds(pl.multiple_of(column * panel, panel), panel)])
        near_ref[:, c * panel : (c + 1) * panel] = jnp.dot(
            jnp.concatenate(picked, axis=1),
            blocks_ref[c].reshape(near_count * panel, panel),
            preferred_element_type=jnp.float32,
        )


def middle_kernel(first, place_ref, columns_ref, sources_ref, blocks_ref, near_ref):
    near_products(columns_ref, sources_ref, near_ref, blocks_ref, first, place_ref[1])


def edge_kernel(first, place_ref, columns_ref, sources_ref, inner_ref, outer_ref, blocks_ref, near_ref, window):
    width = inner_ref.shape[1]
    panels = sources_ref.shape[1]
    panel = blocks_ref.shape[2]
    reach = window.shape[1] - width
    is_left = first == 0
    halo = slice(0, width) if is_left else slice(reach, reach + width)
    own = slice(width, width + reach) if is_left else slice(0, reach)
    source = slice(0, reach) if is_left else slice(panels - reach, panels)
    base = place_ref[1] - width // panel if is_left else place_ref[1] + (panels - reach) // panel
    window[:, own] = sources_ref[:, source]
    from_inner = place_ref[0] == (1 if is_left else 0)

    @pl.when(from_inner)
    def _():
        window[:, halo] = inner_ref[...]

    @pl.when(jnp.logical_not(from_inner))
    def _():
        window[:, halo] = outer_ref[...]

    near_products(columns_ref, window, near_ref, blocks_ref, first, base)


def near_quarter(place, columns, sources, beside, blocks, index, name):
    rhs, panels = sources.shape
    clusters, near_count, panel, _ = blocks.shape
    quarter = clusters // QUARTERS
    smem = pl.BlockSpec(memory_space=pltpu.SMEM)
    vmem = pl.BlockSpec(memory_space=pltpu.VMEM)
    kernel = functools.partial(edge_kernel if beside else middle_kernel, index * quarter)
    scratch = []
    if beside:
        scratch = [pltpu.VMEM((rhs, panels // QUARTERS + 2 * beside[0].shape[1]), sources.dtype)]
    return pl.pallas_call(
        kernel,
        in_specs=[smem, smem] + [vmem] * (2 + len(beside)),
        out_specs=vmem,
        out_shape=jax.ShapeDtypeStruct((rhs, panels // QUARTERS), jnp.float32),
        scratch_shapes=scratch,
        compiler_params=pltpu.CompilerParams(vmem_limit_bytes=NEAR_VMEM_BYTES),
        cost_estimate=pl.CostEstimate(
            flops=2 * rhs * panels * near_count * panel // QUARTERS,
            bytes_accessed=(2 * panels * near_count * panel + 6 * rhs * panels) // QUARTERS,
            transcendentals=0,
        ),
        name=name,
    )(place, columns, sources, *beside, blocks[index * quarter : (index + 1) * quarter])


def far_kernel(
    partial_ref, last_ref, matrix_ref, left_ref, early_ref, late_ref, right_ref, basis_ref, out_ref, leaf_local
):
    step = pl.program_id(0)

    @pl.when(step == 0)
    def _():
        descended = partial_ref[...] + lax.dot_general(
            matrix_ref[...], last_ref[...], TN, precision=highest, preferred_element_type=jnp.float32
        )
        leaf_local[...] = descended.T.astype(leaf_local.dtype)

    clusters, _, panel = basis_ref.shape
    width = left_ref.shape[1]
    flat = jnp.concatenate([basis_ref[c] for c in range(clusters)], axis=1)
    far = jnp.dot(leaf_local[...], flat, preferred_element_type=jnp.float32)

    def put(low, high):
        out_ref[:, :width] = low[...] + far[:, :width]
        out_ref[:, width:] = high[...] + far[:, width:]

    pl.when(step == 0)(lambda: put(left_ref, early_ref))
    pl.when(step != 0)(lambda: put(late_ref, right_ref))


def add_far(partial, last, matrix, left, early, late, right, basis):
    rhs, quarter = left.shape
    clusters, rank, panel = basis.shape
    half_panels = clusters * panel // HALVES
    whole = lambda i: (0, 0)
    return pl.pallas_call(
        far_kernel,
        grid=(HALVES,),
        in_specs=[
            pl.BlockSpec((rank, rhs), whole),
            pl.BlockSpec((rank, rhs), whole),
            pl.BlockSpec((rank, rank), whole),
            *[pl.BlockSpec((rhs, quarter), whole)] * 4,
            pl.BlockSpec((clusters // HALVES, rank, panel), lambda i: (i, 0, 0)),
        ],
        out_specs=pl.BlockSpec((rhs, half_panels), lambda i: (0, i)),
        out_shape=jax.ShapeDtypeStruct((rhs, HALVES * half_panels), jnp.float32),
        scratch_shapes=[pltpu.VMEM((rhs, rank), jnp.bfloat16)],
        compiler_params=pltpu.CompilerParams(vmem_limit_bytes=VMEM_BYTES),
        cost_estimate=pl.CostEstimate(
            flops=4 * rhs * half_panels * rank,
            bytes_accessed=16 * rhs * half_panels + 4 * rank * half_panels,
            transcendentals=0,
        ),
        name="add_far",
    )(partial, last, matrix, left, early, late, right, basis)


def matmul(left, right):
    return jnp.dot(left, right, precision=highest, preferred_element_type=jnp.float32)


def matmul_tn(left, right):
    return lax.dot_general(left, right, TN, precision=highest, preferred_element_type=jnp.float32)


def pick_rows(table, rows):
    one_hot = (rows[:, None] == jnp.arange(table.shape[0], dtype=rows.dtype)[None, :]).astype(table.dtype)
    return jnp.einsum("nkj,sn->skj", table, one_hot, preferred_element_type=jnp.float32)


def together(*values):
    return lax.optimization_barrier(values)


def body(sources, near_blocks, near_cols, basis, transfer, coupling):
    own_clusters = near_blocks.shape[0]
    panel_size = near_blocks.shape[2]
    leaf_count = lax.axis_size("leaf")
    levels = leaf_count.bit_length() - 1
    leaf_index = lax.axis_index("leaf")
    device = lax.axis_index(AXES)
    odd = jnp.bitwise_and(device, 1).astype(jnp.int32)
    odd_flag = odd.reshape(1)
    first_cluster = device * own_clusters

    def place(side, first_column):
        return jnp.stack([side, first_column]).astype(jnp.int32)

    here = place(odd, first_cluster)
    columns = near_cols.T

    level_index = jnp.arange(levels, dtype=jnp.int32)
    node = jnp.right_shift(leaf_index, level_index)
    first_row = jnp.right_shift(leaf_count, level_index) - 2
    mine_rows = (first_row + node).astype(jnp.int32)
    their_rows = (first_row + (node ^ 1)).astype(jnp.int32)

    moment, inner_send, outer_send = moments(odd_flag, sources, basis, REACH * panel_size)

    inner_clusters = inner_exchange(inner_send)
    other = xor_permute(moment, "blk", 1)
    moves = pick_rows(transfer, jnp.concatenate([mine_rows[: levels - 1], their_rows[: levels - 1]]))
    other, moves = together(other, moves)
    current = moment + other

    current, coupling = together(current, coupling)
    other = xor_permute(current, "blk", 3)
    couples = pick_rows(coupling, mine_rows)
    other, couples, inner_clusters = together(other, couples, inner_clusters)
    current = current + other

    siblings = []
    down = [couples[0]]
    chain = moves[0].T
    for level, mask in enumerate([1, 2, 4, 12, 16, 48]):
        if level == 1:
            current, early_sources, early_blocks = together(current, sources, near_blocks)
        elif level == 3:
            current, late_sources, late_blocks = together(current, sources, near_blocks)
        elif level == 2:
            current, outer_send = together(current, outer_send)
        elif level == 4:
            current, left_sources, left_blocks = together(current, sources, near_blocks)
        elif level == 5:
            current, right_sources, right_blocks = together(current, sources, near_blocks)
        sibling = xor_permute(current, "leaf", mask)
        if level == 1:
            early = near_quarter(here, columns, early_sources, (), early_blocks, 1, "near_early")
            sibling, early = together(sibling, early)
        elif level == 3:
            late = near_quarter(here, columns, late_sources, (), late_blocks, 2, "near_late")
            sibling, late, outer_clusters = together(sibling, late, outer_clusters)
        elif level == 2:
            outer_clusters = outer_exchange(outer_send)
        elif level == 4:
            beside = (inner_clusters, outer_clusters)
            left = near_quarter(here, columns, left_sources, beside, left_blocks, 0, "near_left")
            sibling, left = together(sibling, left)
        elif level == 5:
            beside = (inner_clusters, outer_clusters)
            right = near_quarter(here, columns, right_sources, beside, right_blocks, 3, "near_right")
            sibling, right = together(sibling, right)
        siblings.append(sibling)
        if level + 1 < levels:
            current = matmul_tn(moves[level], current) + matmul_tn(moves[levels - 1 + level], sibling)
    for step in range(1, levels):
        chain = chain if step == 1 else matmul_tn(moves[step - 1], chain)
        down.append(matmul(couples[step], chain))
    collected = matmul_tn(jnp.concatenate(down[:-1]), jnp.concatenate(siblings[:-1]))
    return add_far(collected, sibling, down[-1], left, early, late, right, basis)


def solution(mesh):
    return jax.shard_map(
        body,
        mesh=mesh,
        in_specs=(
            P(None, ("leaf", "blk")),
            P(("leaf", "blk"), None, None, None),
            P(("leaf", "blk"), None),
            P(("leaf", "blk"), None, None),
            P(),
            P(),
        ),
        out_specs=P(None, ("leaf", "blk")),
        check_vma=False,
    )
```

```python
import functools

import jax
import jax.numpy as jnp
import numpy as np
from jax import lax
from jax.experimental import pallas as pl
from jax.experimental.pallas import tpu as pltpu
from jax.sharding import PartitionSpec as P

REACH = 4
QUARTERS = 4
VMEM_BYTES = 16 * 1024 * 1024
NEAR_VMEM_BYTES = 16 * 1024 * 1024
MOMENT_VMEM_BYTES = 54784 * 1024

highest = lax.Precision.HIGHEST
AXES = ("leaf", "blk")
NT = (((1,), (1,)), ((), ()))
TN = (((0,), (0,)), ((), ()))


def xor_permute(value, axis, mask):
    pairs = [(source, source ^ mask) for source in range(lax.axis_size(axis))]
    return lax.ppermute(value, axis, pairs)


def inner_exchange(value):
    count = lax.axis_size(AXES)
    return lax.ppermute(value, AXES, [(i, i ^ 1) for i in range(count)])


def outer_exchange(value):
    count = lax.axis_size(AXES)
    pairs = [(i, i + 1) for i in range(1, count - 1, 2)]
    return lax.ppermute(value, AXES, pairs + [(b, a) for a, b in pairs])


def moment_kernel(odd_ref, sources_hbm, basis_hbm, moment_ref, inner_ref, outer_ref, sources, basis, sems):
    chunks = sources.shape[0]
    clusters = basis.shape[0] // chunks
    panels = sources.shape[2]
    width = inner_ref.shape[1]
    copies = []
    for k in range(chunks):
        own = slice(k * clusters, (k + 1) * clusters)
        copies.append(
            (
                pltpu.make_async_copy(
                    sources_hbm.at[:, k * panels : (k + 1) * panels], sources.at[k], sems.at[2 * k]
                ),
                pltpu.make_async_copy(basis_hbm.at[own], basis.at[own], sems.at[2 * k + 1]),
            )
        )
        for copy in copies[-1]:
            copy.start()
    total = jnp.zeros(moment_ref.shape, jnp.float32)
    for k in range(chunks):
        for copy in copies[k]:
            copy.wait()
        flat = jnp.concatenate([basis[k * clusters + c] for c in range(clusters)], axis=1)
        total += lax.dot_general(flat, sources[k], NT, preferred_element_type=jnp.float32)
    moment_ref[...] = total
    odd = odd_ref[0]

    @pl.when(odd == 0)
    def _():
        inner_ref[...] = sources[chunks - 1, :, panels - width :]
        outer_ref[...] = sources[0, :, :width]

    @pl.when(odd != 0)
    def _():
        inner_ref[...] = sources[0, :, :width]
        outer_ref[...] = sources[chunks - 1, :, panels - width :]


def moments(odd, sources, basis, width, chunks=4):
    rhs, panels = sources.shape
    clusters, rank, panel = basis.shape
    vmem = pl.BlockSpec(memory_space=pltpu.VMEM)
    hbm = pl.BlockSpec(memory_space=pltpu.HBM)
    return pl.pallas_call(
        moment_kernel,
        in_specs=[pl.BlockSpec(memory_space=pltpu.SMEM), hbm, hbm],
        out_specs=[vmem] * 3,
        out_shape=[
            jax.ShapeDtypeStruct((rank, rhs), jnp.float32),
            jax.ShapeDtypeStruct((rhs, width), sources.dtype),
            jax.ShapeDtypeStruct((rhs, width), sources.dtype),
        ],
        scratch_shapes=[
            pltpu.VMEM((chunks, rhs, panels // chunks), sources.dtype),
            pltpu.VMEM((clusters, rank, panel), basis.dtype),
            pltpu.SemaphoreType.DMA((2 * chunks,)),
        ],
        compiler_params=pltpu.CompilerParams(vmem_limit_bytes=MOMENT_VMEM_BYTES),
        cost_estimate=pl.CostEstimate(
            flops=2 * rhs * panels * rank, bytes_accessed=2 * panels * (rhs + rank), transcendentals=0
        ),
        name="moments",
    )(odd, sources, basis)


def near_products(columns_ref, panels_ref, near_ref, blocks_ref, first, base):
    quarter_clusters, near_count, panel, _ = blocks_ref.shape
    for c in range(quarter_clusters):
        picked = []
        for slot in range(near_count):
            column = columns_ref[slot, first + c] - base
            picked.append(panels_ref[:, pl.ds(pl.multiple_of(column * panel, panel), panel)])
        near_ref[:, c * panel : (c + 1) * panel] = jnp.dot(
            jnp.concatenate(picked, axis=1),
            blocks_ref[c].reshape(near_count * panel, panel),
            preferred_element_type=jnp.float32,
        )


def middle_kernel(first, place_ref, columns_ref, sources_ref, blocks_ref, near_ref):
    near_products(columns_ref, sources_ref, near_ref, blocks_ref, first, place_ref[1])


def edge_kernel(first, place_ref, columns_ref, sources_ref, inner_ref, outer_ref, blocks_ref, near_ref, window):
    width = inner_ref.shape[1]
    panels = sources_ref.shape[1]
    panel = blocks_ref.shape[2]
    reach = window.shape[1] - width
    is_left = first == 0
    halo = slice(0, width) if is_left else slice(reach, reach + width)
    own = slice(width, width + reach) if is_left else slice(0, reach)
    source = slice(0, reach) if is_left else slice(panels - reach, panels)
    base = place_ref[1] - width // panel if is_left else place_ref[1] + (panels - reach) // panel
    window[:, own] = sources_ref[:, source]
    from_inner = place_ref[0] == (1 if is_left else 0)

    @pl.when(from_inner)
    def _():
        window[:, halo] = inner_ref[...]

    @pl.when(jnp.logical_not(from_inner))
    def _():
        window[:, halo] = outer_ref[...]

    near_products(columns_ref, window, near_ref, blocks_ref, first, base)


def take_quarter(blocks, index):
    quarter = blocks.shape[0] // QUARTERS
    return blocks[index * quarter : (index + 1) * quarter]


def near_quarter(place, columns, sources, beside, blocks, index, name):
    rhs, panels = sources.shape
    quarter, near_count, panel, _ = blocks.shape
    smem = pl.BlockSpec(memory_space=pltpu.SMEM)
    vmem = pl.BlockSpec(memory_space=pltpu.VMEM)
    kernel = functools.partial(edge_kernel if beside else middle_kernel, index * quarter)
    scratch = []
    if beside:
        scratch = [pltpu.VMEM((rhs, panels // QUARTERS + 2 * beside[0].shape[1]), sources.dtype)]
    return pl.pallas_call(
        kernel,
        in_specs=[smem, smem] + [vmem] * (2 + len(beside)),
        out_specs=vmem,
        out_shape=jax.ShapeDtypeStruct((rhs, panels // QUARTERS), jnp.float32),
        scratch_shapes=scratch,
        compiler_params=pltpu.CompilerParams(vmem_limit_bytes=NEAR_VMEM_BYTES),
        cost_estimate=pl.CostEstimate(
            flops=2 * rhs * panels * near_count * panel // QUARTERS,
            bytes_accessed=(2 * panels * near_count * panel + 6 * rhs * panels) // QUARTERS,
            transcendentals=0,
        ),
        name=name,
    )(place, columns, sources, *beside, blocks)


def far_kernel(count, partial_ref, *refs):
    left_ref, early_ref, late_ref, right_ref, basis_ref, out_hbm, total, sems = refs[2 * count :]
    descended = partial_ref[...]
    for value_ref, matrix_ref in zip(refs[:count], refs[count : 2 * count]):
        descended += lax.dot_general(
            matrix_ref[...], value_ref[...], TN, precision=highest, preferred_element_type=jnp.float32
        )
    leaf_local = descended.T.astype(basis_ref.dtype)
    clusters = basis_ref.shape[0] // QUARTERS
    panels = left_ref.shape[1]
    copies = []
    for k, near_ref in enumerate((left_ref, early_ref, late_ref, right_ref)):
        flat = jnp.concatenate([basis_ref[k * clusters + c] for c in range(clusters)], axis=1)
        total[k] = near_ref[...] + jnp.dot(leaf_local, flat, preferred_element_type=jnp.float32)
        copy = pltpu.make_async_copy(total.at[k], out_hbm.at[:, k * panels : (k + 1) * panels], sems.at[k])
        copy.start()
        copies.append(copy)
    for copy in copies:
        copy.wait()


def add_far(partial, last, matrices, left, early, late, right, basis):
    rhs, quarter = left.shape
    rank = basis.shape[1]
    vmem = pl.BlockSpec(memory_space=pltpu.VMEM)
    return pl.pallas_call(
        functools.partial(far_kernel, len(last)),
        in_specs=[vmem] * (6 + 2 * len(last)),
        out_specs=pl.BlockSpec(memory_space=pltpu.HBM),
        out_shape=jax.ShapeDtypeStruct((rhs, QUARTERS * quarter), jnp.float32),
        scratch_shapes=[
            pltpu.VMEM((QUARTERS, rhs, quarter), jnp.float32),
            pltpu.SemaphoreType.DMA((QUARTERS,)),
        ],
        compiler_params=pltpu.CompilerParams(vmem_limit_bytes=VMEM_BYTES),
        cost_estimate=pl.CostEstimate(
            flops=2 * rhs * QUARTERS * quarter * rank,
            bytes_accessed=QUARTERS * (8 * rhs * quarter + 2 * rank * quarter),
            transcendentals=0,
        ),
        name="add_far",
    )(partial, *last, *matrices, left, early, late, right, basis)


def matmul(left, right):
    return jnp.dot(left, right, precision=highest, preferred_element_type=jnp.float32)


def matmul_tn(left, right):
    return lax.dot_general(left, right, TN, precision=highest, preferred_element_type=jnp.float32)


def pick_rows(table, rows):
    one_hot = (rows[:, None] == jnp.arange(table.shape[0], dtype=rows.dtype)[None, :]).astype(table.dtype)
    return jnp.einsum("nkj,sn->skj", table, one_hot, preferred_element_type=jnp.float32)


def together(*values):
    return lax.optimization_barrier(values)


def body(sources, near_blocks, near_cols, basis, transfer, coupling):
    own_clusters = near_blocks.shape[0]
    panel_size = near_blocks.shape[2]
    leaf_count = lax.axis_size("leaf")
    levels = leaf_count.bit_length() - 1
    leaf_index = lax.axis_index("leaf")
    device = lax.axis_index(AXES)
    odd = jnp.bitwise_and(device, 1).astype(jnp.int32)
    odd_flag = odd.reshape(1)
    first_cluster = device * own_clusters

    def place(side, first_column):
        return jnp.stack([side, first_column]).astype(jnp.int32)

    here = place(odd, first_cluster)
    columns = near_cols.T

    below_top = levels - 2
    shifts = np.array([*range(levels - 1), *range(below_top), below_top, below_top], np.int32)
    flips = np.array([0] * (levels - 1) + [1] * below_top + [3, 2], np.int32)
    rows = ((leaf_count >> shifts) - 2) + (jnp.right_shift(leaf_index, shifts) ^ flips)
    rows = rows.astype(jnp.int32)
    mine_shifts = np.arange(levels, dtype=np.int32)
    mine_rows = ((leaf_count >> mine_shifts) - 2) + jnp.right_shift(leaf_index, mine_shifts)
    mine_rows = mine_rows.astype(jnp.int32)

    moment, inner_send, outer_send = moments(odd_flag, sources, basis, REACH * panel_size)

    inner_clusters = inner_exchange(inner_send)
    other = xor_permute(moment, "blk", 1)
    moves = pick_rows(transfer, rows)
    other, moves = together(other, moves)
    current = moment + other

    current, coupling = together(current, coupling)
    other = xor_permute(current, "blk", 3)
    couples = pick_rows(coupling, mine_rows)
    other, couples, inner_clusters = together(other, couples, inner_clusters)
    current = current + other

    chains = [moves[0].T]
    for step in range(1, levels - 1):
        chains.append(matmul_tn(moves[step], chains[-1]))
    down = [couples[0]]
    for step in range(1, below_top - 1):
        down.append(matmul(couples[step], chains[step - 1]))

    siblings = []
    for level, mask in enumerate([1, 2, 4, 12]):
        if level == 1:
            current, early_blocks = together(current, near_blocks)
        elif level == 2:
            current, outer_send = together(current, outer_send)
            current, middle_sources = together(current, sources)
        elif level == 3:
            current, late_sources, middle_blocks = together(current, sources, near_blocks)
        sibling = xor_permute(current, "leaf", mask)
        ready = current
        extras = []
        if level == 1:
            extras.append(take_quarter(early_blocks, 1))
            ready, early_quarter, top_couples, top_chains = together(
                current, *extras, couples[below_top - 1 :], chains[below_top - 2 :]
            )
            tops = [matmul(couple, top) for couple, top in zip(top_couples, top_chains)]
            cousins = [matmul(moves[levels - 1 + below_top + k], tops[-1]) for k in range(2)]
            extras = [early_quarter, *tops, *cousins]
        elif level == 2:
            outer_clusters = outer_exchange(outer_send)
            extras.append(
                near_quarter(here, columns, middle_sources, (), early_quarter, 1, "near_early")
            )
        elif level == 3:
            beside = (inner_clusters, outer_clusters)
            late = near_quarter(here, columns, late_sources, (), take_quarter(middle_blocks, 2), 2, "near_late")
            extras.append(late)
            ready, *extras = together(current, *extras)
            left = near_quarter(here, columns, late_sources, beside, take_quarter(middle_blocks, 0), 0, "near_left")
            extras.append(left)
        extras.append(matmul_tn(moves[level], ready))
        sibling, *extras = together(sibling, *extras)
        if level == 1:
            early_quarter = extras[0]
            down += extras[1:4]
            cousins = extras[4:6]
        elif level == 2:
            early = extras[0]
        elif level == 3:
            late, left = extras[:2]
        siblings.append(sibling)
        current = extras[-1] + matmul_tn(moves[levels - 1 + level], sibling)

    current, last_sources, last_blocks = together(current, sources, near_blocks)
    last = [xor_permute(current, "leaf", mask) for mask in (16, 48, 32)]
    right = near_quarter(here, columns, last_sources, beside, take_quarter(last_blocks, 3), 3, "near_right")
    collected = matmul_tn(jnp.concatenate(down[:below_top]), jnp.concatenate(siblings))
    *last, right, collected = together(*last, right, collected)
    return add_far(collected, last, [down[below_top], *cousins], left, early, late, right, basis)


def solution(mesh):
    return jax.shard_map(
        body,
        mesh=mesh,
        in_specs=(
            P(None, ("leaf", "blk")),
            P(("leaf", "blk"), None, None, None),
            P(("leaf", "blk"), None),
            P(("leaf", "blk"), None, None),
            P(),
            P(),
        ),
        out_specs=P(None, ("leaf", "blk")),
        check_vma=False,
    )
```

```python
import functools

import jax
import jax.numpy as jnp
import numpy as np
from jax import lax
from jax.experimental import pallas as pl
from jax.experimental.pallas import tpu as pltpu
from jax.sharding import PartitionSpec as P

REACH = 4
PIECES = {"left": (0, 8), "middle": (8, 16), "right": (24, 8)}
VMEM_BYTES = 16 * 1024 * 1024
NEAR_VMEM_BYTES = 16 * 1024 * 1024
MOMENT_VMEM_BYTES = 54784 * 1024

highest = lax.Precision.HIGHEST
AXES = ("leaf", "blk")
NT = (((1,), (1,)), ((), ()))
TN = (((0,), (0,)), ((), ()))


def device_index():
    return lax.axis_index("leaf") * lax.axis_size("blk") + lax.axis_index("blk")


def xor_permute(value, axis, mask):
    pairs = [(source, source ^ mask) for source in range(lax.axis_size(axis))]
    return lax.ppermute(value, axis, pairs)


def inner_exchange(value):
    count = lax.axis_size(AXES)
    return lax.ppermute(value, AXES, [(i, i ^ 1) for i in range(count)])


def outer_exchange(value):
    count = lax.axis_size(AXES)
    pairs = [(i, i + 1) for i in range(1, count - 1, 2)]
    return lax.ppermute(value, AXES, pairs + [(b, a) for a, b in pairs])


def moment_kernel(sources_hbm, basis_hbm, moment_ref, inner_ref, outer_ref, sources, basis, sems):
    chunks = sources.shape[0]
    clusters = basis.shape[0] // chunks
    panels = sources.shape[2]
    width = inner_ref.shape[1]
    copies = []
    for k in range(chunks):
        own = slice(k * clusters, (k + 1) * clusters)
        copies.append(
            (
                pltpu.make_async_copy(
                    sources_hbm.at[:, k * panels : (k + 1) * panels], sources.at[k], sems.at[2 * k]
                ),
                pltpu.make_async_copy(basis_hbm.at[own], basis.at[own], sems.at[2 * k + 1]),
            )
        )
        for copy in copies[-1]:
            copy.start()
    total = jnp.zeros(moment_ref.shape, jnp.float32)
    for k in range(chunks):
        for copy in copies[k]:
            copy.wait()
        flat = jnp.concatenate([basis[k * clusters + c] for c in range(clusters)], axis=1)
        total += lax.dot_general(flat, sources[k], NT, preferred_element_type=jnp.float32)
    moment_ref[...] = total
    odd = lax.rem(device_index(), 2)

    @pl.when(odd == 0)
    def _():
        inner_ref[...] = sources[chunks - 1, :, panels - width :]
        outer_ref[...] = sources[0, :, :width]

    @pl.when(odd != 0)
    def _():
        inner_ref[...] = sources[0, :, :width]
        outer_ref[...] = sources[chunks - 1, :, panels - width :]


def moments(sources, basis, width, chunks=4):
    rhs, panels = sources.shape
    clusters, rank, panel = basis.shape
    vmem = pl.BlockSpec(memory_space=pltpu.VMEM)
    hbm = pl.BlockSpec(memory_space=pltpu.HBM)
    return pl.pallas_call(
        moment_kernel,
        in_specs=[hbm, hbm],
        out_specs=[vmem] * 3,
        out_shape=[
            jax.ShapeDtypeStruct((rank, rhs), jnp.float32),
            jax.ShapeDtypeStruct((rhs, width), sources.dtype),
            jax.ShapeDtypeStruct((rhs, width), sources.dtype),
        ],
        scratch_shapes=[
            pltpu.VMEM((chunks, rhs, panels // chunks), sources.dtype),
            pltpu.VMEM((clusters, rank, panel), basis.dtype),
            pltpu.SemaphoreType.DMA((2 * chunks,)),
        ],
        compiler_params=pltpu.CompilerParams(vmem_limit_bytes=MOMENT_VMEM_BYTES),
        cost_estimate=pl.CostEstimate(
            flops=2 * rhs * panels * rank, bytes_accessed=2 * panels * (rhs + rank), transcendentals=0
        ),
        name="moments",
    )(sources, basis)


def near_products(columns_ref, panels_ref, near_ref, blocks_ref, first, base):
    quarter_clusters, near_count, panel, _ = blocks_ref.shape
    for c in range(quarter_clusters):
        picked = []
        for slot in range(near_count):
            column = columns_ref[slot, first + c] - base
            picked.append(panels_ref[:, pl.ds(pl.multiple_of(column * panel, panel), panel)])
        near_ref[:, c * panel : (c + 1) * panel] = jnp.dot(
            jnp.concatenate(picked, axis=1),
            blocks_ref[c].reshape(near_count * panel, panel),
            preferred_element_type=jnp.float32,
        )


def middle_kernel(first, own_clusters, columns_ref, sources_ref, blocks_ref, near_ref):
    near_products(columns_ref, sources_ref, near_ref, blocks_ref, first, device_index() * own_clusters)


def edge_kernel(
    own_clusters,
    columns_ref,
    sources_ref,
    inner_ref,
    outer_ref,
    left_blocks,
    right_blocks,
    left_ref,
    right_ref,
    left_window,
    right_window,
):
    width = inner_ref.shape[1]
    panels = sources_ref.shape[1]
    panel = left_blocks.shape[2]
    reach = left_window.shape[1] - width
    device = device_index()
    odd = lax.rem(device, 2)
    left_window[:, width:] = sources_ref[:, :reach]
    right_window[:, :reach] = sources_ref[:, panels - reach :]

    @pl.when(odd == 0)
    def _():
        left_window[:, :width] = outer_ref[...]
        right_window[:, reach:] = inner_ref[...]

    @pl.when(odd != 0)
    def _():
        left_window[:, :width] = inner_ref[...]
        right_window[:, reach:] = outer_ref[...]

    first = device * own_clusters
    near_products(columns_ref, left_window, left_ref, left_blocks, 0, first - width // panel)
    near_products(
        columns_ref,
        right_window,
        right_ref,
        right_blocks,
        PIECES["right"][0],
        first + (panels - reach) // panel,
    )


def take(blocks, piece):
    first, count = piece
    return blocks[first : first + count]


def near_pieces(columns, sources, beside, blocks, name):
    rhs, panels = sources.shape
    _, near_count, panel, _ = blocks[0].shape
    smem = pl.BlockSpec(memory_space=pltpu.SMEM)
    vmem = pl.BlockSpec(memory_space=pltpu.VMEM)
    widths = [piece.shape[0] * panel for piece in blocks]
    if beside:
        kernel = functools.partial(edge_kernel, panels // panel)
        halo = beside[0].shape[1]
        scratch = [pltpu.VMEM((rhs, width + 2 * halo), sources.dtype) for width in widths]
    else:
        kernel = functools.partial(middle_kernel, PIECES["middle"][0], panels // panel)
        scratch = []
    return pl.pallas_call(
        kernel,
        in_specs=[smem] + [vmem] * (1 + len(beside) + len(blocks)),
        out_specs=[vmem] * len(blocks),
        out_shape=[jax.ShapeDtypeStruct((rhs, width), jnp.float32) for width in widths],
        scratch_shapes=scratch,
        compiler_params=pltpu.CompilerParams(vmem_limit_bytes=NEAR_VMEM_BYTES),
        cost_estimate=pl.CostEstimate(
            flops=2 * rhs * sum(widths) * near_count * panel,
            bytes_accessed=sum(widths) * (2 * near_count * panel + 6 * rhs),
            transcendentals=0,
        ),
        name=name,
    )(columns, sources, *beside, *blocks)


def far_kernel(count, partial_ref, *refs):
    *near_refs, basis_ref, out_hbm, total, sems = refs[2 * count :]
    descended = partial_ref[...]
    for value_ref, matrix_ref in zip(refs[:count], refs[count : 2 * count]):
        descended += lax.dot_general(
            matrix_ref[...], value_ref[...], TN, precision=highest, preferred_element_type=jnp.float32
        )
    leaf_local = descended.T.astype(basis_ref.dtype)
    panel = basis_ref.shape[2]
    copies = []
    start = 0
    for k, near_ref in enumerate(near_refs):
        own = slice(start, start + near_ref.shape[1])
        start = own.stop
        flat = jnp.concatenate([basis_ref[c] for c in range(own.start // panel, own.stop // panel)], axis=1)
        total[:, own] = near_ref[...] + jnp.dot(leaf_local, flat, preferred_element_type=jnp.float32)
        copy = pltpu.make_async_copy(total.at[:, own], out_hbm.at[:, own], sems.at[k])
        copy.start()
        copies.append(copy)
    for copy in copies:
        copy.wait()


def add_far(partial, last, matrices, near, basis):
    rhs = partial.shape[1]
    clusters, rank, panel = basis.shape
    vmem = pl.BlockSpec(memory_space=pltpu.VMEM)
    return pl.pallas_call(
        functools.partial(far_kernel, len(last)),
        in_specs=[vmem] * (2 + 2 * len(last) + len(near)),
        out_specs=pl.BlockSpec(memory_space=pltpu.HBM),
        out_shape=jax.ShapeDtypeStruct((rhs, clusters * panel), jnp.float32),
        scratch_shapes=[
            pltpu.VMEM((rhs, clusters * panel), jnp.float32),
            pltpu.SemaphoreType.DMA((len(near),)),
        ],
        compiler_params=pltpu.CompilerParams(vmem_limit_bytes=VMEM_BYTES),
        cost_estimate=pl.CostEstimate(
            flops=2 * rhs * clusters * panel * rank,
            bytes_accessed=clusters * panel * (8 * rhs + 2 * rank),
            transcendentals=0,
        ),
        name="add_far",
    )(partial, *last, *matrices, *near, basis)


def matmul(left, right):
    return jnp.dot(left, right, precision=highest, preferred_element_type=jnp.float32)


def matmul_tn(left, right):
    return lax.dot_general(left, right, TN, precision=highest, preferred_element_type=jnp.float32)


def pick_rows(table, rows):
    one_hot = (rows[:, None] == jnp.arange(table.shape[0], dtype=rows.dtype)[None, :]).astype(table.dtype)
    return jnp.einsum("nkj,sn->skj", table, one_hot, preferred_element_type=jnp.float32)


def together(*values):
    return lax.optimization_barrier(values)


def body(sources, near_blocks, near_cols, basis, transfer, coupling):
    panel_size = near_blocks.shape[2]
    leaf_count = lax.axis_size("leaf")
    levels = leaf_count.bit_length() - 1
    leaf_index = lax.axis_index("leaf")
    columns = near_cols.T

    below_top = levels - 2
    shifts = np.array([*range(levels - 1), *range(below_top), below_top, below_top], np.int32)
    flips = np.array([0] * (levels - 1) + [1] * below_top + [3, 2], np.int32)
    rows = ((leaf_count >> shifts) - 2) + (jnp.right_shift(leaf_index, shifts) ^ flips)
    rows = rows.astype(jnp.int32)
    mine_shifts = np.arange(levels, dtype=np.int32)
    mine_rows = ((leaf_count >> mine_shifts) - 2) + jnp.right_shift(leaf_index, mine_shifts)
    mine_rows = mine_rows.astype(jnp.int32)

    moment, inner_send, outer_send = moments(sources, basis, REACH * panel_size)

    inner_clusters = inner_exchange(inner_send)
    other = xor_permute(moment, "blk", 1)
    moves = pick_rows(transfer, rows)
    other, moves = together(other, moves)
    current = moment + other

    current, coupling = together(current, coupling)
    other = xor_permute(current, "blk", 3)
    couples = pick_rows(coupling, mine_rows)
    other, couples, inner_clusters = together(other, couples, inner_clusters)
    current = current + other

    chains = [moves[0].T]
    for step in range(1, levels - 1):
        chains.append(matmul_tn(moves[step], chains[-1]))
    down = [couples[0]]
    for step in range(1, below_top - 1):
        down.append(matmul(couples[step], chains[step - 1]))

    siblings = []
    for level, mask in enumerate([1, 2, 4, 12]):
        if level == 1:
            current, middle_blocks = together(current, near_blocks)
        elif level == 2:
            current, middle_sources = together(current, sources)
        elif level == 3:
            current, outer_send = together(current, outer_send)
        sibling = xor_permute(current, "leaf", mask)
        ready = current
        extras = []
        if level == 1:
            mine, middle_blocks = together(matmul_tn(moves[level], current), middle_blocks)
            extras = [take(middle_blocks, PIECES["middle"]), mine]
        elif level == 2:
            (middle,) = near_pieces(columns, middle_sources, (), [middle_blocks], "near_middle")
            ready, middle, top_couples, top_chains = together(
                current, middle, couples[below_top - 1 :], chains[below_top - 2 :]
            )
            tops = [matmul(couple, top) for couple, top in zip(top_couples, top_chains)]
            cousins = [matmul(moves[levels - 1 + below_top + k], tops[-1]) for k in range(2)]
            extras = [middle, *tops, *cousins]
        elif level == 3:
            outer_clusters = outer_exchange(outer_send)
        if level != 1:
            extras.append(matmul_tn(moves[level], ready))
        sibling, *extras = together(sibling, *extras)
        if level == 1:
            middle_blocks = extras[0]
        elif level == 2:
            middle = extras[0]
            down += extras[1:4]
            cousins = extras[4:6]
        siblings.append(sibling)
        current = extras[-1] + matmul_tn(moves[levels - 1 + level], sibling)

    current, last_sources, last_blocks = together(current, sources, near_blocks)
    last = [xor_permute(current, "leaf", mask) for mask in (16, 48, 32)]
    left, right = near_pieces(
        columns,
        last_sources,
        (inner_clusters, outer_clusters),
        [take(last_blocks, PIECES["left"]), take(last_blocks, PIECES["right"])],
        "near_edges",
    )
    collected = matmul_tn(jnp.concatenate(down[:below_top]), jnp.concatenate(siblings))
    *last, left, right, collected = together(*last, left, right, collected)
    return add_far(collected, last, [down[below_top], *cousins], [left, middle, right], basis)


def solution(mesh):
    return jax.shard_map(
        body,
        mesh=mesh,
        in_specs=(
            P(None, ("leaf", "blk")),
            P(("leaf", "blk"), None, None, None),
            P(("leaf", "blk"), None),
            P(("leaf", "blk"), None, None),
            P(),
            P(),
        ),
        out_specs=P(None, ("leaf", "blk")),
        check_vma=False,
    )
```

```python
import functools

import jax
import jax.numpy as jnp
import numpy as np
from jax import lax
from jax.experimental import pallas as pl
from jax.experimental.pallas import tpu as pltpu
from jax.sharding import PartitionSpec as P

REACH = 4
PIECES = {"left": (0, 8), "middle": (8, 16), "right": (24, 8)}
VMEM_BYTES = 16 * 1024 * 1024
NEAR_VMEM_BYTES = 16 * 1024 * 1024
MOMENT_VMEM_BYTES = 54784 * 1024

highest = lax.Precision.HIGHEST
AXES = ("leaf", "blk")
NT = (((1,), (1,)), ((), ()))
TN = (((0,), (0,)), ((), ()))


def device_index():
    return lax.axis_index("leaf") * lax.axis_size("blk") + lax.axis_index("blk")


def xor_permute(value, axis, mask):
    pairs = [(source, source ^ mask) for source in range(lax.axis_size(axis))]
    return lax.ppermute(value, axis, pairs)


def inner_exchange(value):
    count = lax.axis_size(AXES)
    return lax.ppermute(value, AXES, [(i, i ^ 1) for i in range(count)])


def outer_exchange(value):
    count = lax.axis_size(AXES)
    pairs = [(i, i + 1) for i in range(1, count - 1, 2)]
    return lax.ppermute(value, AXES, pairs + [(b, a) for a, b in pairs])


def moment_kernel(sources_hbm, basis_hbm, moment_ref, inner_ref, outer_ref, sources, basis, sems):
    chunks = sources.shape[0]
    clusters = basis.shape[0] // chunks
    panels = sources.shape[2]
    width = inner_ref.shape[1]
    copies = []
    for k in range(chunks):
        own = slice(k * clusters, (k + 1) * clusters)
        copies.append(
            (
                pltpu.make_async_copy(
                    sources_hbm.at[:, k * panels : (k + 1) * panels], sources.at[k], sems.at[2 * k]
                ),
                pltpu.make_async_copy(basis_hbm.at[own], basis.at[own], sems.at[2 * k + 1]),
            )
        )
        for copy in copies[-1]:
            copy.start()
    total = jnp.zeros(moment_ref.shape, jnp.float32)
    for k in range(chunks):
        for copy in copies[k]:
            copy.wait()
        flat = jnp.concatenate([basis[k * clusters + c] for c in range(clusters)], axis=1)
        total += lax.dot_general(flat, sources[k], NT, preferred_element_type=jnp.float32)
    moment_ref[...] = total
    odd = lax.rem(device_index(), 2)

    @pl.when(odd == 0)
    def _():
        inner_ref[...] = sources[chunks - 1, :, panels - width :]
        outer_ref[...] = sources[0, :, :width]

    @pl.when(odd != 0)
    def _():
        inner_ref[...] = sources[0, :, :width]
        outer_ref[...] = sources[chunks - 1, :, panels - width :]


def moments(sources, basis, width, chunks=2):
    rhs, panels = sources.shape
    clusters, rank, panel = basis.shape
    vmem = pl.BlockSpec(memory_space=pltpu.VMEM)
    hbm = pl.BlockSpec(memory_space=pltpu.HBM)
    return pl.pallas_call(
        moment_kernel,
        in_specs=[hbm, hbm],
        out_specs=[vmem] * 3,
        out_shape=[
            jax.ShapeDtypeStruct((rank, rhs), jnp.float32),
            jax.ShapeDtypeStruct((rhs, width), sources.dtype),
            jax.ShapeDtypeStruct((rhs, width), sources.dtype),
        ],
        scratch_shapes=[
            pltpu.VMEM((chunks, rhs, panels // chunks), sources.dtype),
            pltpu.VMEM((clusters, rank, panel), basis.dtype),
            pltpu.SemaphoreType.DMA((2 * chunks,)),
        ],
        compiler_params=pltpu.CompilerParams(vmem_limit_bytes=MOMENT_VMEM_BYTES),
        cost_estimate=pl.CostEstimate(
            flops=2 * rhs * panels * rank, bytes_accessed=2 * panels * (rhs + rank), transcendentals=0
        ),
        name="moments",
    )(sources, basis)


def near_products(columns_ref, panels_ref, near_ref, blocks_ref, first, base):
    quarter_clusters, near_count, panel, _ = blocks_ref.shape
    for c in range(quarter_clusters):
        picked = []
        for slot in range(near_count):
            column = columns_ref[slot, first + c] - base
            picked.append(panels_ref[:, pl.ds(pl.multiple_of(column * panel, panel), panel)])
        near_ref[:, c * panel : (c + 1) * panel] = jnp.dot(
            jnp.concatenate(picked, axis=1),
            blocks_ref[c].reshape(near_count * panel, panel),
            preferred_element_type=jnp.float32,
        )


def middle_kernel(first, own_clusters, columns_ref, sources_ref, blocks_ref, near_ref):
    near_products(columns_ref, sources_ref, near_ref, blocks_ref, first, device_index() * own_clusters)


def edge_kernel(
    own_clusters,
    columns_ref,
    sources_ref,
    inner_ref,
    outer_ref,
    left_blocks,
    right_blocks,
    left_ref,
    right_ref,
    left_window,
    right_window,
):
    width = inner_ref.shape[1]
    panels = sources_ref.shape[1]
    panel = left_blocks.shape[2]
    reach = left_window.shape[1] - width
    device = device_index()
    odd = lax.rem(device, 2)
    left_window[:, width:] = sources_ref[:, :reach]
    right_window[:, :reach] = sources_ref[:, panels - reach :]

    @pl.when(odd == 0)
    def _():
        left_window[:, :width] = outer_ref[...]
        right_window[:, reach:] = inner_ref[...]

    @pl.when(odd != 0)
    def _():
        left_window[:, :width] = inner_ref[...]
        right_window[:, reach:] = outer_ref[...]

    first = device * own_clusters
    near_products(columns_ref, left_window, left_ref, left_blocks, 0, first - width // panel)
    near_products(
        columns_ref,
        right_window,
        right_ref,
        right_blocks,
        PIECES["right"][0],
        first + (panels - reach) // panel,
    )


def take(blocks, piece):
    first, count = piece
    return blocks[first : first + count]


def near_pieces(columns, sources, beside, blocks, name):
    rhs, panels = sources.shape
    _, near_count, panel, _ = blocks[0].shape
    smem = pl.BlockSpec(memory_space=pltpu.SMEM)
    vmem = pl.BlockSpec(memory_space=pltpu.VMEM)
    widths = [piece.shape[0] * panel for piece in blocks]
    if beside:
        kernel = functools.partial(edge_kernel, panels // panel)
        halo = beside[0].shape[1]
        scratch = [pltpu.VMEM((rhs, width + 2 * halo), sources.dtype) for width in widths]
    else:
        kernel = functools.partial(middle_kernel, PIECES["middle"][0], panels // panel)
        scratch = []
    return pl.pallas_call(
        kernel,
        in_specs=[smem] + [vmem] * (1 + len(beside) + len(blocks)),
        out_specs=[vmem] * len(blocks),
        out_shape=[jax.ShapeDtypeStruct((rhs, width), jnp.float32) for width in widths],
        scratch_shapes=scratch,
        compiler_params=pltpu.CompilerParams(vmem_limit_bytes=NEAR_VMEM_BYTES),
        cost_estimate=pl.CostEstimate(
            flops=2 * rhs * sum(widths) * near_count * panel,
            bytes_accessed=sum(widths) * (2 * near_count * panel + 6 * rhs),
            transcendentals=0,
        ),
        name=name,
    )(columns, sources, *beside, *blocks)


def far_kernel(count, partial_ref, *refs):
    *near_refs, basis_ref, out_hbm, total, sems = refs[2 * count :]
    values = jnp.concatenate([ref[...] for ref in refs[:count]], axis=0)
    matrices = jnp.concatenate([ref[...] for ref in refs[count : 2 * count]], axis=0)
    descended = partial_ref[...] + lax.dot_general(
        matrices, values, TN, precision=highest, preferred_element_type=jnp.float32
    )
    leaf_local = descended.T.astype(basis_ref.dtype)
    panel = basis_ref.shape[2]
    copies = []
    start = 0
    for k, near_ref in enumerate(near_refs):
        own = slice(start, start + near_ref.shape[1])
        start = own.stop
        flat = jnp.concatenate([basis_ref[c] for c in range(own.start // panel, own.stop // panel)], axis=1)
        total[:, own] = near_ref[...] + jnp.dot(leaf_local, flat, preferred_element_type=jnp.float32)
        copy = pltpu.make_async_copy(total.at[:, own], out_hbm.at[:, own], sems.at[k])
        copy.start()
        copies.append(copy)
    for copy in copies:
        copy.wait()


def add_far(partial, last, matrices, near, basis):
    rhs = partial.shape[1]
    clusters, rank, panel = basis.shape
    vmem = pl.BlockSpec(memory_space=pltpu.VMEM)
    return pl.pallas_call(
        functools.partial(far_kernel, len(last)),
        in_specs=[vmem] * (2 + 2 * len(last) + len(near)),
        out_specs=pl.BlockSpec(memory_space=pltpu.HBM),
        out_shape=jax.ShapeDtypeStruct((rhs, clusters * panel), jnp.float32),
        scratch_shapes=[
            pltpu.VMEM((rhs, clusters * panel), jnp.float32),
            pltpu.SemaphoreType.DMA((len(near),)),
        ],
        compiler_params=pltpu.CompilerParams(vmem_limit_bytes=VMEM_BYTES),
        cost_estimate=pl.CostEstimate(
            flops=2 * rhs * clusters * panel * rank,
            bytes_accessed=clusters * panel * (8 * rhs + 2 * rank),
            transcendentals=0,
        ),
        name="add_far",
    )(partial, *last, *matrices, *near, basis)


def matmul(left, right):
    return jnp.dot(left, right, precision=highest, preferred_element_type=jnp.float32)


def matmul_tn(left, right):
    return lax.dot_general(left, right, TN, precision=highest, preferred_element_type=jnp.float32)


def pick_rows(table, rows):
    one_hot = (rows[:, None] == jnp.arange(table.shape[0], dtype=rows.dtype)[None, :]).astype(table.dtype)
    return jnp.einsum("nkj,sn->skj", table, one_hot, preferred_element_type=jnp.float32)


def together(*values):
    return lax.optimization_barrier(values)


def body(sources, near_blocks, near_cols, basis, transfer, coupling):
    panel_size = near_blocks.shape[2]
    leaf_count = lax.axis_size("leaf")
    levels = leaf_count.bit_length() - 1
    leaf_index = lax.axis_index("leaf")
    columns = near_cols.T

    below_top = levels - 2
    shifts = np.array([*range(levels - 1), *range(below_top), below_top, below_top], np.int32)
    flips = np.array([0] * (levels - 1) + [1] * below_top + [3, 2], np.int32)
    rows = ((leaf_count >> shifts) - 2) + (jnp.right_shift(leaf_index, shifts) ^ flips)
    rows = rows.astype(jnp.int32)
    mine_shifts = np.arange(levels, dtype=np.int32)
    mine_rows = ((leaf_count >> mine_shifts) - 2) + jnp.right_shift(leaf_index, mine_shifts)
    mine_rows = mine_rows.astype(jnp.int32)

    moment, inner_send, outer_send = moments(sources, basis, REACH * panel_size)

    inner_clusters = inner_exchange(inner_send)
    other = xor_permute(moment, "blk", 1)
    moves = pick_rows(transfer, rows)
    other, moves = together(other, moves)
    current = moment + other

    current, coupling = together(current, coupling)
    other = xor_permute(current, "blk", 3)
    couples = pick_rows(coupling, mine_rows)
    other, couples, inner_clusters = together(other, couples, inner_clusters)
    current = current + other

    chains = [moves[0].T]
    for step in range(1, levels - 1):
        chains.append(matmul_tn(moves[step], chains[-1]))
    down = [couples[0]]
    for step in range(1, below_top - 1):
        down.append(matmul(couples[step], chains[step - 1]))

    siblings = []
    for level, mask in enumerate([1, 2, 4, 12]):
        if level == 1:
            current, middle_blocks = together(current, near_blocks)
        elif level == 2:
            current, middle_sources = together(current, sources)
        elif level == 3:
            current, outer_send = together(current, outer_send)
        sibling = xor_permute(current, "leaf", mask)
        ready = current
        extras = []
        if level == 1:
            mine, middle_blocks = together(matmul_tn(moves[level], current), middle_blocks)
            extras = [take(middle_blocks, PIECES["middle"]), mine]
        elif level == 2:
            (middle,) = near_pieces(columns, middle_sources, (), [middle_blocks], "near_middle")
            ready, middle, top_couples, top_chains = together(
                current, middle, couples[below_top - 1 :], chains[below_top - 2 :]
            )
            tops = [matmul(couple, top) for couple, top in zip(top_couples, top_chains)]
            cousins = [matmul(moves[levels - 1 + below_top + k], tops[-1]) for k in range(2)]
            extras = [middle, *tops, *cousins]
        elif level == 3:
            outer_clusters = outer_exchange(outer_send)
        if level != 1:
            extras.append(matmul_tn(moves[level], ready))
        sibling, *extras = together(sibling, *extras)
        if level == 1:
            middle_blocks = extras[0]
        elif level == 2:
            middle = extras[0]
            down += extras[1:4]
            cousins = extras[4:6]
        siblings.append(sibling)
        current = extras[-1] + matmul_tn(moves[levels - 1 + level], sibling)

    current, last_sources, last_blocks = together(current, sources, near_blocks)
    last = [xor_permute(current, "leaf", mask) for mask in (16, 48, 32)]
    left, right = near_pieces(
        columns,
        last_sources,
        (inner_clusters, outer_clusters),
        [take(last_blocks, PIECES["left"]), take(last_blocks, PIECES["right"])],
        "near_edges",
    )
    collected = matmul_tn(jnp.concatenate(down[:below_top]), jnp.concatenate(siblings))
    *last, left, right, collected = together(*last, left, right, collected)
    return add_far(collected, last, [down[below_top], *cousins], [left, middle, right], basis)


def solution(mesh):
    return jax.shard_map(
        body,
        mesh=mesh,
        in_specs=(
            P(None, ("leaf", "blk")),
            P(("leaf", "blk"), None, None, None),
            P(("leaf", "blk"), None),
            P(("leaf", "blk"), None, None),
            P(),
            P(),
        ),
        out_specs=P(None, ("leaf", "blk")),
        check_vma=False,
    )
```

```python
import functools

import jax
import jax.numpy as jnp
import numpy as np
from jax import lax
from jax.experimental import pallas as pl
from jax.experimental.pallas import tpu as pltpu
from jax.sharding import PartitionSpec as P

REACH = 4
PIECES = {"left": (0, 8), "middle": (8, 16), "right": (24, 8)}
VMEM_BYTES = 16 * 1024 * 1024
NEAR_VMEM_BYTES = 16 * 1024 * 1024
MOMENT_VMEM_BYTES = 54784 * 1024

highest = lax.Precision.HIGHEST
AXES = ("leaf", "blk")
NT = (((1,), (1,)), ((), ()))
TN = (((0,), (0,)), ((), ()))


def device_index():
    return lax.axis_index("leaf") * lax.axis_size("blk") + lax.axis_index("blk")


def xor_permute(value, axis, mask):
    pairs = [(source, source ^ mask) for source in range(lax.axis_size(axis))]
    return lax.ppermute(value, axis, pairs)


def inner_exchange(value):
    count = lax.axis_size(AXES)
    return lax.ppermute(value, AXES, [(i, i ^ 1) for i in range(count)])


def outer_exchange(value):
    count = lax.axis_size(AXES)
    pairs = [(i, i + 1) for i in range(1, count - 1, 2)]
    return lax.ppermute(value, AXES, pairs + [(b, a) for a, b in pairs])


def moment_kernel(sources_hbm, basis_hbm, moment_ref, inner_ref, outer_ref, sources, basis, sems):
    chunks = sources.shape[0]
    clusters = basis.shape[0] // chunks
    panels = sources.shape[2]
    width = inner_ref.shape[1]
    copies = []
    for k in range(chunks):
        own = slice(k * clusters, (k + 1) * clusters)
        copies.append(
            (
                pltpu.make_async_copy(
                    sources_hbm.at[:, k * panels : (k + 1) * panels], sources.at[k], sems.at[2 * k]
                ),
                pltpu.make_async_copy(basis_hbm.at[own], basis.at[own], sems.at[2 * k + 1]),
            )
        )
        for copy in copies[-1]:
            copy.start()
    total = jnp.zeros(moment_ref.shape, jnp.float32)
    for k in range(chunks):
        for copy in copies[k]:
            copy.wait()
        flat = jnp.concatenate([basis[k * clusters + c] for c in range(clusters)], axis=1)
        total += lax.dot_general(flat, sources[k], NT, preferred_element_type=jnp.float32)
    moment_ref[...] = total
    odd = lax.rem(device_index(), 2)

    @pl.when(odd == 0)
    def _():
        inner_ref[...] = sources[chunks - 1, :, panels - width :]
        outer_ref[...] = sources[0, :, :width]

    @pl.when(odd != 0)
    def _():
        inner_ref[...] = sources[0, :, :width]
        outer_ref[...] = sources[chunks - 1, :, panels - width :]


def moments(sources, basis, width, chunks=2):
    rhs, panels = sources.shape
    clusters, rank, panel = basis.shape
    vmem = pl.BlockSpec(memory_space=pltpu.VMEM)
    hbm = pl.BlockSpec(memory_space=pltpu.HBM)
    return pl.pallas_call(
        moment_kernel,
        in_specs=[hbm, hbm],
        out_specs=[vmem] * 3,
        out_shape=[
            jax.ShapeDtypeStruct((rank, rhs), jnp.float32),
            jax.ShapeDtypeStruct((rhs, width), sources.dtype),
            jax.ShapeDtypeStruct((rhs, width), sources.dtype),
        ],
        scratch_shapes=[
            pltpu.VMEM((chunks, rhs, panels // chunks), sources.dtype),
            pltpu.VMEM((clusters, rank, panel), basis.dtype),
            pltpu.SemaphoreType.DMA((2 * chunks,)),
        ],
        compiler_params=pltpu.CompilerParams(vmem_limit_bytes=MOMENT_VMEM_BYTES),
        cost_estimate=pl.CostEstimate(
            flops=2 * rhs * panels * rank, bytes_accessed=2 * panels * (rhs + rank), transcendentals=0
        ),
        name="moments",
    )(sources, basis)


def near_products(columns_ref, panels_ref, near_ref, blocks_ref, first, base):
    quarter_clusters, near_count, panel, _ = blocks_ref.shape
    for c in range(quarter_clusters):
        picked = []
        for slot in range(near_count):
            column = columns_ref[slot, first + c] - base
            picked.append(panels_ref[:, pl.ds(pl.multiple_of(column * panel, panel), panel)])
        near_ref[:, c * panel : (c + 1) * panel] = jnp.dot(
            jnp.concatenate(picked, axis=1),
            blocks_ref[c].reshape(near_count * panel, panel),
            preferred_element_type=jnp.float32,
        )


def middle_kernel(first, own_clusters, columns_ref, sources_ref, blocks_ref, near_ref):
    near_products(columns_ref, sources_ref, near_ref, blocks_ref, first, device_index() * own_clusters)


def edge_kernel(
    own_clusters,
    columns_ref,
    sources_ref,
    inner_ref,
    outer_ref,
    left_blocks,
    right_blocks,
    left_ref,
    right_ref,
    left_window,
    right_window,
):
    width = inner_ref.shape[1]
    panels = sources_ref.shape[1]
    panel = left_blocks.shape[2]
    reach = left_window.shape[1] - width
    device = device_index()
    odd = lax.rem(device, 2)
    left_window[:, width:] = sources_ref[:, :reach]
    right_window[:, :reach] = sources_ref[:, panels - reach :]

    @pl.when(odd == 0)
    def _():
        left_window[:, :width] = outer_ref[...]
        right_window[:, reach:] = inner_ref[...]

    @pl.when(odd != 0)
    def _():
        left_window[:, :width] = inner_ref[...]
        right_window[:, reach:] = outer_ref[...]

    first = device * own_clusters
    near_products(columns_ref, left_window, left_ref, left_blocks, 0, first - width // panel)
    near_products(
        columns_ref,
        right_window,
        right_ref,
        right_blocks,
        PIECES["right"][0],
        first + (panels - reach) // panel,
    )


def take(blocks, piece):
    first, count = piece
    return blocks[first : first + count]


def near_pieces(columns, sources, beside, blocks, name):
    rhs, panels = sources.shape
    _, near_count, panel, _ = blocks[0].shape
    smem = pl.BlockSpec(memory_space=pltpu.SMEM)
    vmem = pl.BlockSpec(memory_space=pltpu.VMEM)
    widths = [piece.shape[0] * panel for piece in blocks]
    if beside:
        kernel = functools.partial(edge_kernel, panels // panel)
        halo = beside[0].shape[1]
        scratch = [pltpu.VMEM((rhs, width + 2 * halo), sources.dtype) for width in widths]
    else:
        kernel = functools.partial(middle_kernel, PIECES["middle"][0], panels // panel)
        scratch = []
    return pl.pallas_call(
        kernel,
        in_specs=[smem] + [vmem] * (1 + len(beside) + len(blocks)),
        out_specs=[vmem] * len(blocks),
        out_shape=[jax.ShapeDtypeStruct((rhs, width), jnp.float32) for width in widths],
        scratch_shapes=scratch,
        compiler_params=pltpu.CompilerParams(vmem_limit_bytes=NEAR_VMEM_BYTES),
        cost_estimate=pl.CostEstimate(
            flops=2 * rhs * sum(widths) * near_count * panel,
            bytes_accessed=sum(widths) * (2 * near_count * panel + 6 * rhs),
            transcendentals=0,
        ),
        name=name,
    )(columns, sources, *beside, *blocks)


def far_kernel(count, partial_ref, *refs):
    *near_refs, basis_ref, out_hbm, total, sems = refs[2 * count :]
    values = jnp.concatenate([ref[...] for ref in refs[:count]], axis=0)
    matrices = jnp.concatenate([ref[...] for ref in refs[count : 2 * count]], axis=0)
    descended = partial_ref[...] + lax.dot_general(
        matrices, values, TN, precision=highest, preferred_element_type=jnp.float32
    )
    leaf_local = descended.T.astype(basis_ref.dtype)
    panel = basis_ref.shape[2]
    copies = []
    start = 0
    for k, near_ref in enumerate(near_refs):
        own = slice(start, start + near_ref.shape[1])
        start = own.stop
        flat = jnp.concatenate([basis_ref[c] for c in range(own.start // panel, own.stop // panel)], axis=1)
        total[:, own] = near_ref[...] + jnp.dot(leaf_local, flat, preferred_element_type=jnp.float32)
        copy = pltpu.make_async_copy(total.at[:, own], out_hbm.at[:, own], sems.at[k])
        copy.start()
        copies.append(copy)
    for copy in copies:
        copy.wait()


def add_far(partial, last, matrices, near, basis):
    rhs = partial.shape[1]
    clusters, rank, panel = basis.shape
    vmem = pl.BlockSpec(memory_space=pltpu.VMEM)
    return pl.pallas_call(
        functools.partial(far_kernel, len(last)),
        in_specs=[vmem] * (2 + 2 * len(last) + len(near)),
        out_specs=pl.BlockSpec(memory_space=pltpu.HBM),
        out_shape=jax.ShapeDtypeStruct((rhs, clusters * panel), jnp.float32),
        scratch_shapes=[
            pltpu.VMEM((rhs, clusters * panel), jnp.float32),
            pltpu.SemaphoreType.DMA((len(near),)),
        ],
        compiler_params=pltpu.CompilerParams(vmem_limit_bytes=VMEM_BYTES),
        cost_estimate=pl.CostEstimate(
            flops=2 * rhs * clusters * panel * rank,
            bytes_accessed=clusters * panel * (8 * rhs + 2 * rank),
            transcendentals=0,
        ),
        name="add_far",
    )(partial, *last, *matrices, *near, basis)


def matmul(left, right):
    return jnp.dot(left, right, precision=highest, preferred_element_type=jnp.float32)


def matmul_tn(left, right):
    return lax.dot_general(left, right, TN, precision=highest, preferred_element_type=jnp.float32)


def pick_rows(table, rows):
    one_hot = (rows[:, None] == jnp.arange(table.shape[0], dtype=rows.dtype)[None, :]).astype(table.dtype)
    return jnp.einsum("nkj,sn->skj", table, one_hot, preferred_element_type=jnp.float32)


def together(*values):
    return lax.optimization_barrier(values)


def body(sources, near_blocks, near_cols, basis, transfer, coupling):
    panel_size = near_blocks.shape[2]
    leaf_count = lax.axis_size("leaf")
    levels = leaf_count.bit_length() - 1
    leaf_index = lax.axis_index("leaf")
    columns = near_cols.T

    below_top = levels - 2
    shifts = np.array([*range(levels - 1), *range(below_top), below_top, below_top], np.int32)
    flips = np.array([0] * (levels - 1) + [1] * below_top + [3, 2], np.int32)
    rows = ((leaf_count >> shifts) - 2) + (jnp.right_shift(leaf_index, shifts) ^ flips)
    rows = rows.astype(jnp.int32)
    mine_shifts = np.arange(levels, dtype=np.int32)
    mine_rows = ((leaf_count >> mine_shifts) - 2) + jnp.right_shift(leaf_index, mine_shifts)
    mine_rows = mine_rows.astype(jnp.int32)

    moment, inner_send, outer_send = moments(sources, basis, REACH * panel_size)

    inner_clusters = inner_exchange(inner_send)
    other = xor_permute(moment, "blk", 1)
    moves = pick_rows(transfer, rows)
    other, moves = together(other, moves)
    current = moment + other

    current, coupling = together(current, coupling)
    other = xor_permute(current, "blk", 3)
    couples = pick_rows(coupling, mine_rows)
    other, couples, inner_clusters = together(other, couples, inner_clusters)
    current = current + other

    chains = [moves[0].T]
    for step in range(1, levels - 1):
        chains.append(matmul_tn(moves[step], chains[-1]))
    down = [couples[0]]
    for step in range(1, below_top - 1):
        down.append(matmul(couples[step], chains[step - 1]))

    siblings = []
    for level, mask in enumerate([1, 2, 4, 14]):
        if level == 1:
            current, middle_blocks = together(current, near_blocks)
        elif level == 2:
            current, middle_sources = together(current, sources)
        elif level == 3:
            current, outer_send = together(current, outer_send)
        sibling = xor_permute(current, "leaf", mask)
        ready = current
        extras = []
        if level == 1:
            mine, middle_blocks = together(matmul_tn(moves[level], current), middle_blocks)
            extras = [take(middle_blocks, PIECES["middle"]), mine]
        elif level == 2:
            (middle,) = near_pieces(columns, middle_sources, (), [middle_blocks], "near_middle")
            ready, middle, top_couples, top_chains = together(
                current, middle, couples[below_top - 1 :], chains[below_top - 2 :]
            )
            tops = [matmul(couple, top) for couple, top in zip(top_couples, top_chains)]
            cousins = [matmul(moves[levels - 1 + below_top + k], tops[-1]) for k in range(2)]
            extras = [middle, *tops, *cousins]
        elif level == 3:
            outer_clusters = outer_exchange(outer_send)
        if level != 1:
            extras.append(matmul_tn(moves[level], ready))
        sibling, *extras = together(sibling, *extras)
        if level == 1:
            middle_blocks = extras[0]
        elif level == 2:
            middle = extras[0]
            down += extras[1:4]
            cousins = extras[4:6]
        siblings.append(sibling)
        current = extras[-1] + matmul_tn(moves[levels - 1 + level], sibling)

    current, last_sources, last_blocks = together(current, sources, near_blocks)
    last = [xor_permute(current, "leaf", mask) for mask in (16, 48, 32)]
    left, right = near_pieces(
        columns,
        last_sources,
        (inner_clusters, outer_clusters),
        [take(last_blocks, PIECES["left"]), take(last_blocks, PIECES["right"])],
        "near_edges",
    )
    collected = matmul_tn(jnp.concatenate(down[:below_top]), jnp.concatenate(siblings))
    *last, left, right, collected = together(*last, left, right, collected)
    return add_far(collected, last, [down[below_top], *cousins], [left, middle, right], basis)


def solution(mesh):
    return jax.shard_map(
        body,
        mesh=mesh,
        in_specs=(
            P(None, ("leaf", "blk")),
            P(("leaf", "blk"), None, None, None),
            P(("leaf", "blk"), None),
            P(("leaf", "blk"), None, None),
            P(),
            P(),
        ),
        out_specs=P(None, ("leaf", "blk")),
        check_vma=False,
    )
```
